512 devices in a mesh: seq: 64 (over z, x), tp: 8 (over y, core).
Axes of the slice: x: 4, y: 4, z: 16, core: 2. Of those that a mesh axis runs over, the one named last changes fastest.
Arguments:
- tokens: bfloat16 [131072, 1280], P(('seq', 'tp')), may hold values from -48 to 48
- slot_embed: bfloat16 [64, 1280], replicated, may hold values from -1 to 1
- w_in: bfloat16 [64, 1280, 2560], P('seq', None, 'tp'), may hold values from -0.15625 to 0.15625
- w_out: bfloat16 [64, 2560, 1280], P('seq', 'tp'), may hold values from -0.125 to 0.125
- cotangent: bfloat16 [131072, 1280], P(('seq', 'tp')), may hold values from -6 to 6
Outputs:
- layer_output: bfloat16 [131072, 1280], P(('seq', 'tp'))
- grad_tokens: bfloat16 [131072, 1280], P(('seq', 'tp'))
- grad_embed: float32 [64, 1280], P('seq', 'tp')
The draws below stay inside these ranges and needn't reach their ends.
All inputs are finite; a program needn't handle non-finite values.
Results may differ from the reference program's by a relative error of at most 0.023.
Values may be sent and summed in bfloat16 or wider, within the bound.
A program may use at most 64 MiB of HBM per device.

```python
import math
import jax
import jax.numpy as jnp
from jax import lax

D = 1280
FF = 2560
PATCHES = 256
IMAGES = 512
EXPERTS = 64
TOKENS = 131072
N_TP = 8


def common_embed(key):
    gauss_part = jax.random.normal(key, (EXPERTS, D), jnp.float32) * D ** (-0.5)
    return gauss_part


def draw_slot_embed(key, part):
    slot_rows = common_embed(key)
    return jnp.clip(slot_rows, -1.0, 1.0).astype(jnp.bfloat16)


def draw_tokens(key, part):
    key = jax.random.fold_in(key, 11)
    key_list = jax.random.split(key, 3)
    positions = jnp.arange(TOKENS, dtype=jnp.float32)
    rising = (0.5 + positions / TOKENS)[:, None]
    roughness = jnp.exp(jax.random.uniform(key_list[0], (TOKENS, 1), jnp.float32, -0.35, 0.35))
    feature_scale = jnp.exp(jax.random.uniform(key_list[1], (1, D), jnp.float32, 0.0, math.log(10.0))) / 4.6
    values = jax.random.normal(key_list[2], (TOKENS, D), jnp.float32) * rising * roughness * feature_scale
    return jnp.clip(values, -48.0, 48.0).astype(jnp.bfloat16)


def block_scale(key, shape, pieces, low, high):
    loudness = 1.0
    for axis_at, shards_of in pieces:
        steps = jax.random.uniform(jax.random.fold_in(jax.random.fold_in(key, 6), axis_at), (shards_of,), jnp.float32, low / len(pieces), high / len(pieces))
        loudness = loudness * jnp.repeat(jnp.exp(steps), shape[axis_at] // shards_of).reshape((-1,) + (1,) * (len(shape) - 1 - axis_at))
    return loudness


def normal_values(own_key, shape, width, bound, shards=(), kind=jnp.bfloat16):
    loudness = block_scale(own_key, shape, shards, -0.22, 0.18) if shards else 1.0
    entries = jax.random.normal(own_key, shape, jnp.float32) * width * loudness
    return jnp.minimum(jnp.maximum(entries, -bound), bound).astype(kind)


def setup_inputs(seed: int = 0) -> dict:
    seeds = jax.random.split(jax.random.key(seed), 6)
    tokens = draw_tokens(jax.random.fold_in(seeds[5], 71), 0)
    slot_embed = draw_slot_embed(jax.random.fold_in(seeds[5], 71), 0)
    w_in = normal_values(seeds[2], (EXPERTS, D, FF), D ** -0.5, 0.15625, ((0, 64), (2, 8)))
    w_out = normal_values(seeds[3], (EXPERTS, FF, D), FF ** -0.5, 0.125, ((0, 64), (1, 8)))
    cotangent = normal_values(seeds[4], (TOKENS, D), 1.0, 6.0, ((0, 512),))
    return dict(tokens=tokens, slot_embed=slot_embed, w_in=w_in, w_out=w_out, cotangent=cotangent)


def normalize_rows(values):
    return values * lax.rsqrt(lax.optimization_barrier(jnp.mean(values * values, axis=-1, keepdims=True)) + 1e-06)

def block_sum(first_operand, second_operand):
    block_width = first_operand.shape[1] // N_TP
    running = jnp.zeros((first_operand.shape[0], second_operand.shape[1]), jnp.float32)
    for block_index in range(N_TP):
        lower = block_index * block_width
        piece_sum = jnp.dot(first_operand[:, lower:lower + block_width], second_operand[lower:lower + block_width], preferred_element_type=jnp.float32).astype(jnp.bfloat16)
        piece_sum = lax.optimization_barrier(piece_sum)
        running = running + piece_sum.astype(jnp.float32)
    return running

def expert_forward(operands):
    slot_rows, weight_in, weight_out = operands
    preact = jnp.dot(slot_rows, weight_in, preferred_element_type=jnp.float32)
    hidden = jax.nn.gelu(preact).astype(jnp.bfloat16)
    return block_sum(hidden, weight_out)

def expert_backward(operands):
    slot_rows, grad_rows, weight_in, weight_out = operands
    preact = jnp.dot(slot_rows, weight_in, preferred_element_type=jnp.float32)
    grad_hidden = jnp.dot(grad_rows, weight_out.T, preferred_element_type=jnp.float32)
    unused_value, gelu_pullback = jax.vjp(jax.nn.gelu, preact)
    grad_preact = gelu_pullback(grad_hidden)[0].astype(jnp.bfloat16)
    return block_sum(grad_preact, weight_in.T)

def reference(tokens, slot_embed, w_in, w_out, cotangent):
    images = tokens.reshape(IMAGES, PATCHES, D).astype(jnp.float32)
    cot_images = cotangent.reshape(IMAGES, PATCHES, D).astype(jnp.float32)
    embed_wide = slot_embed.astype(jnp.float32)
    logits = jnp.einsum('ipd,ed->ipe', images, embed_wide)
    column_max = lax.optimization_barrier(jnp.max(logits, axis=1, keepdims=True))
    column_exp = jnp.exp(logits - column_max)
    dispatch = column_exp / lax.optimization_barrier(jnp.sum(column_exp, axis=1, keepdims=True))
    dispatch_round = dispatch.astype(jnp.bfloat16)
    slot_inputs = jnp.einsum('ipe,ipd->ied', dispatch_round.astype(jnp.float32), images)
    normed, norm_pullback = jax.vjp(normalize_rows, slot_inputs)
    normed_round = normed.astype(jnp.bfloat16)
    expert_rows = jnp.transpose(normed_round, (1, 0, 2))
    slot_outputs = jnp.transpose(lax.map(expert_forward, (expert_rows, w_in, w_out)).astype(jnp.bfloat16), (1, 0, 2))
    row_max = lax.optimization_barrier(jnp.max(logits, axis=2, keepdims=True))
    row_exp = jnp.exp(logits - row_max)
    combine = row_exp / lax.optimization_barrier(jnp.sum(row_exp, axis=2, keepdims=True))
    combine_round = combine.astype(jnp.bfloat16)
    slot_wide = slot_outputs.astype(jnp.float32)
    layer_output = jnp.einsum('ipe,ied->ipd', combine_round.astype(jnp.float32), slot_wide).astype(jnp.bfloat16)
    grad_combine = jnp.einsum('ipd,ied->ipe', cot_images, slot_wide)
    grad_slot_out = jnp.einsum('ipe,ipd->ied', combine_round.astype(jnp.float32), cot_images).astype(jnp.bfloat16)
    grad_rows = jnp.transpose(grad_slot_out, (1, 0, 2))
    grad_normed = jnp.transpose(lax.map(expert_backward, (expert_rows, grad_rows, w_in, w_out)), (1, 0, 2))
    grad_slot_in = norm_pullback(grad_normed)[0].astype(jnp.bfloat16)
    grad_slot_wide = grad_slot_in.astype(jnp.float32)
    grad_dispatch = jnp.einsum('ipd,ied->ipe', images, grad_slot_wide)
    dispatch_inner = lax.optimization_barrier(jnp.sum(dispatch * grad_dispatch, axis=1, keepdims=True))
    combine_inner = lax.optimization_barrier(jnp.sum(combine * grad_combine, axis=2, keepdims=True))
    grad_logits = (combine * (grad_combine - combine_inner) + dispatch * (grad_dispatch - dispatch_inner)).astype(jnp.bfloat16)
    grad_logits_wide = grad_logits.astype(jnp.float32)
    grad_tokens = (jnp.einsum('ipe,ied->ipd', dispatch_round.astype(jnp.float32), grad_slot_wide) + jnp.einsum('ipe,ed->ipd', grad_logits_wide, embed_wide)).astype(jnp.bfloat16)
    grad_embed = jnp.einsum('ipe,ipd->ed', grad_logits_wide, images)
    return (layer_output.reshape(TOKENS, D), grad_tokens.reshape(TOKENS, D), grad_embed)
```

```python
import jax
import jax.numpy as jnp
from jax import lax
from jax.sharding import PartitionSpec as P

D = 1280
PATCHES = 256


def normalize_rows(values):
    return values * lax.rsqrt(jnp.mean(values * values, axis=-1, keepdims=True) + 1e-06)


def inner_first(first_operand, second_operand):
    return lax.dot_general(
        first_operand, second_operand, (((0,), (0,)), ((), ())), preferred_element_type=jnp.float32
    )


def send_slots(slot_rows):
    moved_rows = lax.all_to_all(slot_rows, "seq", split_axis=1, concat_axis=0, tiled=True)
    return lax.all_gather(moved_rows, "tp", axis=0, tiled=True)


def return_slots(partial_out):
    summed = lax.psum_scatter(
        partial_out.astype(jnp.bfloat16), "tp", scatter_dimension=0, tiled=True
    ).astype(jnp.float32)
    return lax.all_to_all(
        summed.astype(jnp.bfloat16), "seq", split_axis=0, concat_axis=1, tiled=True
    ).astype(summed.dtype)


def shards(tokens, slot_embed, w_in, w_out, cotangent):
    images = tokens.reshape(-1, PATCHES, D)
    cot_images = cotangent.reshape(-1, PATCHES, D)
    logits = jnp.einsum("ipd,ed->ipe", images, slot_embed, preferred_element_type=jnp.float32)
    column_max = jnp.max(logits, axis=1, keepdims=True)
    column_exp = jnp.exp(logits - column_max)
    dispatch = column_exp / jnp.sum(column_exp, axis=1, keepdims=True)
    dispatch_round = dispatch.astype(jnp.bfloat16)
    slot_inputs = jnp.einsum(
        "ipe,ipd->ied", dispatch_round, images, preferred_element_type=jnp.float32
    )
    normed, norm_pullback = jax.vjp(normalize_rows, slot_inputs)
    normed_round = normed.astype(jnp.bfloat16)
    expert_rows = send_slots(normed_round)
    preact = jnp.einsum("red,edf->ref", expert_rows, w_in, preferred_element_type=jnp.float32)
    hidden = jax.nn.gelu(preact).astype(jnp.bfloat16)
    partial_out = jnp.einsum("ref,efd->red", hidden, w_out, preferred_element_type=jnp.float32)
    slot_outputs = return_slots(partial_out).astype(jnp.bfloat16)
    row_max = jnp.max(logits, axis=2, keepdims=True)
    row_exp = jnp.exp(logits - row_max)
    combine = row_exp / jnp.sum(row_exp, axis=2, keepdims=True)
    combine_round = combine.astype(jnp.bfloat16)
    layer_output = jnp.einsum(
        "ipe,ied->ipd", combine_round, slot_outputs, preferred_element_type=jnp.float32
    ).astype(jnp.bfloat16)
    grad_combine = jnp.einsum(
        "ipd,ied->ipe", cot_images, slot_outputs, preferred_element_type=jnp.float32
    )
    grad_slot_out = jnp.einsum(
        "ipe,ipd->ied", combine_round, cot_images, preferred_element_type=jnp.float32
    ).astype(jnp.bfloat16)
    grad_rows = send_slots(grad_slot_out)
    grad_hidden = jnp.einsum("red,efd->ref", grad_rows, w_out, preferred_element_type=jnp.float32)
    unused_value, gelu_pullback = jax.vjp(jax.nn.gelu, preact)
    grad_preact = gelu_pullback(grad_hidden)[0].astype(jnp.bfloat16)
    grad_partial = jnp.einsum("ref,edf->red", grad_preact, w_in, preferred_element_type=jnp.float32)
    grad_normed = return_slots(grad_partial)
    grad_slot_in = norm_pullback(grad_normed)[0].astype(jnp.bfloat16)
    grad_dispatch = jnp.einsum(
        "ipd,ied->ipe", images, grad_slot_in, preferred_element_type=jnp.float32
    )
    dispatch_inner = jnp.sum(dispatch * grad_dispatch, axis=1, keepdims=True)
    combine_inner = jnp.sum(combine * grad_combine, axis=2, keepdims=True)
    grad_logits = (
        combine * (grad_combine - combine_inner) + dispatch * (grad_dispatch - dispatch_inner)
    ).astype(jnp.bfloat16)
    grad_tokens = (
        jnp.einsum("ipe,ied->ipd", dispatch_round, grad_slot_in, preferred_element_type=jnp.float32)
        + jnp.einsum("ipe,ed->ipd", grad_logits, slot_embed, preferred_element_type=jnp.float32)
    ).astype(jnp.bfloat16)
    flat_logits = grad_logits.reshape(tokens.shape[0], -1)
    embed_part = inner_first(flat_logits, tokens)
    embed_tp = lax.psum_scatter(embed_part, "tp", scatter_dimension=1, tiled=True)
    grad_embed = lax.psum_scatter(embed_tp, "seq", scatter_dimension=0, tiled=True)
    return (layer_output.reshape(tokens.shape), grad_tokens.reshape(tokens.shape), grad_embed)


def solution(mesh):
    return jax.shard_map(
        shards,
        mesh=mesh,
        in_specs=(
            P(("seq", "tp"), None),
            P(),
            P("seq", None, "tp"),
            P("seq", "tp", None),
            P(("seq", "tp"), None),
        ),
        out_specs=(P(("seq", "tp"), None), P(("seq", "tp"), None), P("seq", "tp")),
        check_vma=False,
    )
```

```python
import functools
import math

import jax
import jax.numpy as jnp
from jax import lax
from jax.experimental import pallas as pl
from jax.experimental.pallas import tpu as pltpu
from jax.sharding import PartitionSpec as P

X_CHIPS = 4
CORES = 2
WIDE = 256
MESH = pl.DeviceIdType.MESH
F32 = jnp.float32
BF16 = jnp.bfloat16


def dot(a, b, contract=(1, 0)):
    dims = (((contract[0],), (contract[1],)), ((), ()))
    return lax.dot_general(a, b, dims, preferred_element_type=F32)


def one_hot_swap(outer, inner):
    count = outer * inner
    row = lax.broadcasted_iota(jnp.int32, (count, count), 0)
    column = lax.broadcasted_iota(jnp.int32, (count, count), 1)
    o, i = row // inner, row % inner
    return (column == i * outer + o).astype(F32).astype(BF16)


def gelu_and_slope(u):
    k = math.sqrt(2.0 / math.pi)
    th = jnp.tanh(k * (u + 0.044715 * (u * u * u)))
    half = 0.5 * (1.0 + th)
    slope = half + 0.5 * u * (1.0 - th * th) * (k * (1.0 + 3 * 0.044715 * (u * u)))
    return u * half, slope


def far_first(count):
    return sorted(range(1, count), key=lambda d: -min(d, count - d))


def kernel(names, sizes, *refs):
    nz, nx, ny = sizes
    nt = CORES * ny
    r = dict(zip(names, refs))
    seq, t = lax.axis_index("seq"), lax.axis_index("tp")
    z, x = seq // nx, seq % nx
    y, c = t // CORES, t % CORES
    other = 1 - c
    rows = nz * nx
    width = r["slot_in"].shape[1]
    started = []

    def at_z(p):
        return (p * nx + x, t)

    def at_x(p):
        return (z * nx + p, t)

    def at_y(p):
        return (seq, p * CORES + c)

    def at_y_other(p):
        return (seq, p * CORES + other)

    def at_t(p):
        return (seq, p)

    sibling = (seq, y * CORES + other)

    def copy_to(src, dst, sems, k, device):
        return pltpu.make_async_remote_copy(
            src_ref=src,
            dst_ref=dst,
            send_sem=r[sems + "_s"].at[k],
            recv_sem=r[sems + "_r"].at[k],
            device_id=device,
            device_id_type=MESH,
        )

    def start(*args):
        one = copy_to(*args)
        one.start()
        started.append(one)
        return one

    def exchange(src, dst, me, count, device, sems, order=None):
        copies = []
        for k, d in enumerate(order or range(1, count)):
            peer = lax.rem(me + d, count)
            copies.append(start(src.at[peer], dst.at[me], sems, k, device(peer)))
        dst[pl.ds(me, 1)] = src[pl.ds(me, 1)]
        return copies

    def arrive(copies):
        for one in copies:
            one.wait_recv()

    loads = {}
    for k, name in enumerate(("tokens", "cot", "win", "wout")):
        loads[name] = pltpu.make_async_copy(r[name + "_hbm"], r[name], r["load"].at[k])
        loads[name].start()

    barrier = pltpu.get_barrier_semaphore()
    peers = [at_z(lax.rem(z + d, nz)) for d in range(1, nz)]
    peers += [at_x(lax.rem(x + d, nx)) for d in range(1, nx)]
    peers += [at_t(lax.rem(t + d, nt)) for d in range(1, nt)]
    for peer in peers:
        pl.semaphore_signal(barrier, inc=1, device_id=peer, device_id_type=MESH)

    z_order = far_first(nz)
    loads["tokens"].wait()
    logits = dot(r["embed"][...], r["tokens"][...], (1, 1))
    column_exp = jnp.exp(logits - jnp.max(logits, axis=1, keepdims=True))
    dispatch = column_exp / jnp.sum(column_exp, axis=1, keepdims=True)
    r["dispatch"][...] = dispatch
    slot_in = dot(dispatch.astype(BF16), r["tokens"][...])
    r["slot_in"][...] = slot_in
    scale = lax.rsqrt(jnp.mean(slot_in * slot_in, axis=1, keepdims=True) + 1e-06)
    r["z_out_f"][...] = (slot_in * scale).reshape(nz, nx, width).astype(BF16)
    pl.semaphore_wait(barrier, len(peers))
    z_f = exchange(r["z_out_f"], r["z_in_f"], z, nz, at_z, "z_f", z_order)
    row_exp = jnp.exp(logits - jnp.max(logits, axis=0, keepdims=True))
    combine = row_exp / jnp.sum(row_exp, axis=0, keepdims=True)
    r["combine"][...] = combine
    loads["cot"].wait()
    slot_grad = dot(combine.astype(BF16), r["cot"][...])
    r["z_out_b"][...] = slot_grad.reshape(nz, nx, width).astype(BF16)
    z_b = exchange(r["z_out_b"], r["z_in_b"], z, nz, at_z, "z_b", z_order)

    def spread_x(h, copies):
        arrive(copies)
        held = r["z_in_" + h][...].reshape(rows, width)
        r["x_out_" + h][...] = dot(one_hot_swap(nx, nz), held).astype(BF16).reshape(nx, nz, width)
        return exchange(r["x_out_" + h], r["gather_" + h].at[c, y], x, nx, at_x, "x_" + h)

    def gather_start(h, copies):
        arrive(copies)
        block = r["gather_" + h].at[c, y]
        near = start(block, block, "core_" + h, 0, sibling)
        far = []
        for k, d in enumerate(range(1, ny)):
            far.append(start(block, block, "y_" + h, k, at_y(lax.rem(y + d, ny))))
        return near, far

    def gather_pass(h, far):
        near = []
        for k, d in enumerate(range(1, ny)):
            far[k].wait_recv()
            block = r["gather_" + h].at[c, lax.rem(y + ny - d, ny)]
            near.append(start(block, block, "core_" + h, k + 1, sibling))
        return near

    def expert_inner(h, group):
        held = r["gather_" + h][group].reshape(ny * rows, width)
        if h == "f":
            hidden, slope = gelu_and_slope(dot(held, r["win"][...], (1, 1)))
            r["slope"][group] = slope
            return hidden.astype(BF16)
        return (dot(held, r["wout"][...], (1, 1)) * r["slope"][group]).astype(BF16)

    def expert_outer(h, inner, use):
        weight = r["wout"] if h == "f" else r["win"]
        for low in range(0, width, WIDE):
            cols = pl.ds(low, min(WIDE, width - low))
            use(cols, dot(inner, weight[:, cols]).reshape(ny, rows, -1))

    def expert_near(h):
        def use(cols, part):
            r["half_" + h][:, :, cols] = part.astype(BF16)

        expert_outer(h, expert_inner(h, c), use)
        return start(r["half_" + h], r["half_in_" + h], "half_" + h, 0, sibling)

    def expert_far(h, half):
        inner = expert_inner(h, other)
        half.wait_recv()

        def use(cols, part):
            pair = part + r["half_in_" + h][:, :, cols].astype(F32)
            r["pair_" + h][:, :, cols] = pair.astype(BF16)

        expert_outer(h, inner, use)
        copies = []
        for k, d in enumerate(range(1, ny)):
            peer = lax.rem(y + d, ny)
            copies.append(start(r["pair_" + h].at[peer], r["sum_" + h].at[y], "sum_" + h, k, at_y_other(peer)))
        copies.append(start(r["pair_" + h].at[y], r["sum_" + h].at[y], "sum_" + h, ny - 1, sibling))
        return copies

    def return_x(h, copies):
        arrive(copies)
        total = r["sum_" + h][0].astype(F32)
        for k in range(1, ny):
            total = total + r["sum_" + h][k].astype(F32)
        r["x_back_" + h][...] = total.astype(BF16).reshape(nx, nz, width)
        return exchange(r["x_back_" + h], r["x_home_" + h], x, nx, at_x, "xh_" + h)

    def return_z(h, copies):
        arrive(copies)
        held = r["x_home_" + h][...].reshape(rows, width)
        r["z_back_" + h][...] = dot(one_hot_swap(nz, nx), held).reshape(nz, nx, width).astype(BF16)
        return exchange(r["z_back_" + h], r["z_home_" + h], z, nz, at_z, "zh_" + h, z_order)

    x_f = spread_x("f", z_f)
    near_f, far_f = gather_start("f", x_f)
    x_b = spread_x("b", z_b)
    near_b, far_b = gather_start("b", x_b)
    loads["win"].wait()
    loads["wout"].wait()
    pass_f = gather_pass("f", far_f)
    half_f = expert_near("f")
    arrive([near_f] + pass_f)
    sum_f = expert_far("f", half_f)
    pass_b = gather_pass("b", far_b)
    half_b = expert_near("b")
    arrive([near_b] + pass_b)
    sum_b = expert_far("b", half_b)
    xh_f = return_x("f", sum_f)
    zh_f = return_z("f", xh_f)
    xh_b = return_x("b", sum_b)
    zh_b = return_z("b", xh_b)

    arrive(zh_f)
    combine = r["combine"][...]
    slot_out = r["z_home_f"][...].reshape(rows, width)
    r["out"][...] = dot(combine.T.astype(BF16), slot_out).astype(BF16)
    store_out = pltpu.make_async_copy(r["out"], r["out_hbm"], r["load"].at[4])
    store_out.start()
    grad_combine = dot(slot_out, r["cot"][...], (1, 1))
    combine_inner = jnp.sum(combine * grad_combine, axis=0, keepdims=True)
    grad_logits = combine * (grad_combine - combine_inner)
    slot_in = r["slot_in"][...]
    scale = lax.rsqrt(jnp.mean(slot_in * slot_in, axis=1, keepdims=True) + 1e-06)
    arrive(zh_b)
    grad_normed = r["z_home_b"][...].reshape(rows, width).astype(F32)
    along = jnp.mean(grad_normed * slot_in, axis=1, keepdims=True)
    grad_slot_in = (scale * grad_normed - slot_in * (scale * scale * scale * along)).astype(BF16)
    dispatch = r["dispatch"][...]
    grad_dispatch = dot(grad_slot_in, r["tokens"][...], (1, 1))
    dispatch_inner = jnp.sum(dispatch * grad_dispatch, axis=1, keepdims=True)
    grad_logits = (grad_logits + dispatch * (grad_dispatch - dispatch_inner)).astype(BF16)

    zl = nz // nt
    embed_part = dot(grad_logits, r["tokens"][...])
    r["ge_t_out"][...] = embed_part.reshape(nt, zl * nx, width)
    ge_t = exchange(r["ge_t_out"], r["ge_t_in"], t, nt, at_t, "ge_t")
    both = jnp.concatenate([dispatch.T.astype(BF16), grad_logits.astype(F32).T.astype(BF16)], axis=1)
    right = jnp.concatenate([grad_slot_in, r["embed"][...]], axis=0)
    r["gtok"][...] = dot(both, right).astype(BF16)
    store_gtok = pltpu.make_async_copy(r["gtok"], r["gtok_hbm"], r["load"].at[5])
    store_gtok.start()
    arrive(ge_t)
    owned = jnp.sum(r["ge_t_in"][...], axis=0)
    for lower in range(zl):
        for p in range(nx):
            r["ge_x_out"][p, lower : lower + 1] = owned[lower * nx + p : lower * nx + p + 1]
    ge_x = exchange(r["ge_x_out"], r["ge_x_in"], x, nx, at_x, "ge_x")
    arrive(ge_x)
    owned = jnp.sum(r["ge_x_in"][...], axis=0)
    to_owner = []
    for lower in range(zl):
        r["ge_z_out"][lower] = owned[lower : lower + 1]
    for lower in range(zl):
        owner = t * zl + lower
        one = pltpu.make_async_remote_copy(
            src_ref=r["ge_z_out"].at[lower],
            dst_ref=r["ge_z_in"].at[z],
            send_sem=r["ge_z_s"].at[lower],
            recv_sem=r["ge_z_r"].at[z],
            device_id=at_z(owner),
            device_id_type=MESH,
        )
        to_owner.append((owner, one))

        @pl.when(owner != z)
        def send():
            one.start()

    shares = []
    for k, d in enumerate(range(1, nt)):
        one = pltpu.make_async_remote_copy(
            src_ref=r["ge_row"],
            dst_ref=r["ge_row"],
            send_sem=r["ge_row_s"].at[k],
            recv_sem=r["ge_row_r"].at[0],
            device_id=at_t(lax.rem(t + d, nt)),
            device_id_type=MESH,
        )
        shares.append(one)
    is_owner = z // zl == t

    @pl.when(is_owner)
    def own():
        r["ge_z_in"][pl.ds(z, 1)] = r["ge_z_out"][pl.ds(z - t * zl, 1)]
        for d in range(1, nz):
            source = lax.rem(z + d, nz)
            pltpu.make_async_remote_copy(
                src_ref=r["ge_z_out"].at[0],
                dst_ref=r["ge_z_in"].at[source],
                send_sem=r["ge_z_s"].at[0],
                recv_sem=r["ge_z_r"].at[source],
                device_id=at_z(source),
                device_id_type=MESH,
            ).wait_recv()
        r["ge_row"][...] = jnp.sum(r["ge_z_in"][...], axis=0)
        for one in shares:
            one.start()

    @pl.when(jnp.logical_not(is_owner))
    def take():
        shares[0].wait_recv()

    row = r["ge_row"][...]
    part = width // nt
    mine = row[:, :part]
    for k in range(1, nt):
        mine = jnp.where(t == k, row[:, k * part : (k + 1) * part], mine)
    r["gemb"][...] = mine

    for owner, one in to_owner:

        @pl.when(owner != z)
        def sent():
            one.wait_send()

    @pl.when(is_owner)
    def shared():
        for one in shares:
            one.wait_send()

    store_out.wait()
    store_gtok.wait()
    for one in started:
        one.wait_send()


def solution(mesh):
    nx = X_CHIPS if mesh.shape["seq"] % X_CHIPS == 0 else 1
    nz = mesh.shape["seq"] // nx
    nt = mesh.shape["tp"]
    ny = nt // CORES
    zl = nz // nt
    rows = nz * nx

    def shards(tokens, slot_embed, w_in, w_out, cotangent):
        patches, width = tokens.shape
        inner = w_out.shape[1]
        vmem, dma = pltpu.VMEM, pltpu.SemaphoreType.DMA
        scratch = dict(
            tokens=vmem((patches, width), BF16),
            cot=vmem((patches, width), BF16),
            win=vmem((inner, width), BF16),
            wout=vmem((inner, width), BF16),
            out=vmem((patches, width), BF16),
            gtok=vmem((patches, width), BF16),
            dispatch=vmem((rows, patches), F32),
            combine=vmem((rows, patches), F32),
            slot_in=vmem((rows, width), F32),
            slope=vmem((CORES, ny * rows, inner), F32),
            ge_t_out=vmem((nt, zl * nx, width), F32),
            ge_t_in=vmem((nt, zl * nx, width), F32),
            ge_x_out=vmem((nx, zl, width), F32),
            ge_x_in=vmem((nx, zl, width), F32),
            ge_z_out=vmem((zl, 1, width), F32),
            ge_z_in=vmem((nz, 1, width), F32),
            ge_row=vmem((1, width), F32),
            load=dma((6,)),
            ge_t_s=dma((nt - 1,)),
            ge_t_r=dma((nt - 1,)),
            ge_x_s=dma((nx - 1,)),
            ge_x_r=dma((nx - 1,)),
            ge_z_s=dma((zl,)),
            ge_z_r=dma((nz,)),
            ge_row_s=dma((nt - 1,)),
            ge_row_r=dma((1,)),
        )
        for h in "fb":
            for name in ("z_out", "z_in", "z_back", "z_home"):
                scratch[name + "_" + h] = vmem((nz, nx, width), BF16)
            for name in ("x_out", "x_back", "x_home"):
                scratch[name + "_" + h] = vmem((nx, nz, width), BF16)
            scratch["gather_" + h] = vmem((CORES, ny, nx, nz, width), BF16)
            for name in ("half", "half_in", "pair", "sum"):
                scratch[name + "_" + h] = vmem((ny, rows, width), BF16)
            counts = dict(z=nz - 1, zh=nz - 1, x=nx - 1, xh=nx - 1, y=ny - 1, core=ny, half=1, sum=ny)
            for name, count in counts.items():
                scratch[name + "_" + h + "_s"] = dma((count,))
                scratch[name + "_" + h + "_r"] = dma((count,))
        ins = ["tokens_hbm", "embed", "win_hbm", "wout_hbm", "cot_hbm"]
        outs = ["out_hbm", "gtok_hbm", "gemb"]
        names = ins + outs + list(scratch)
        anywhere = pl.BlockSpec(memory_space=pl.ANY)
        local = pl.BlockSpec(memory_space=pltpu.VMEM)
        return pl.pallas_call(
            functools.partial(kernel, names, (nz, nx, ny)),
            out_shape=(
                jax.ShapeDtypeStruct(tokens.shape, BF16),
                jax.ShapeDtypeStruct(tokens.shape, BF16),
                jax.ShapeDtypeStruct((1, width // nt), F32),
            ),
            in_specs=[anywhere, local, anywhere, anywhere, anywhere],
            out_specs=(anywhere, anywhere, local),
            scratch_shapes=list(scratch.values()),
            compiler_params=pltpu.CompilerParams(
                collective_id=0, has_side_effects=True, vmem_limit_bytes=48 * 1024 * 1024
            ),
        )(tokens, slot_embed, jnp.swapaxes(w_in[0], 0, 1), w_out[0], cotangent)

    return jax.shard_map(
        shards,
        mesh=mesh,
        in_specs=(
            P(("seq", "tp"), None),
            P(),
            P("seq", None, "tp"),
            P("seq", "tp", None),
            P(("seq", "tp"), None),
        ),
        out_specs=(P(("seq", "tp"), None), P(("seq", "tp"), None), P("seq", "tp")),
        check_vma=False,
    )
```

```python
import functools
import math

import jax
import jax.numpy as jnp
from jax import lax
from jax.experimental import pallas as pl
from jax.experimental.pallas import tpu as pltpu
from jax.sharding import PartitionSpec as P

X_CHIPS = 4
CORES = 2
WIDE = 256
STEPS = 2
MESH = pl.DeviceIdType.MESH
F32 = jnp.float32
BF16 = jnp.bfloat16


def dot(a, b, contract=(1, 0)):
    dims = (((contract[0],), (contract[1],)), ((), ()))
    return lax.dot_general(a, b, dims, preferred_element_type=F32)


def one_hot_swap(outer, inner):
    count = outer * inner
    row = lax.broadcasted_iota(jnp.int32, (count, count), 0)
    column = lax.broadcasted_iota(jnp.int32, (count, count), 1)
    o, i = row // inner, row % inner
    return (column == i * outer + o).astype(F32).astype(BF16)


def gelu_and_slope(u):
    k = math.sqrt(2.0 / math.pi)
    th = jnp.tanh(k * (u + 0.044715 * (u * u * u)))
    half = 0.5 * (1.0 + th)
    slope = half + 0.5 * u * (1.0 - th * th) * (k * (1.0 + 3 * 0.044715 * (u * u)))
    return u * half, slope


def far_first(count):
    return sorted(range(1, count), key=lambda d: -min(d, count - d))


def kernel(names, sizes, *refs):
    nz, nx, ny = sizes
    nt = CORES * ny
    r = dict(zip(names, refs))
    seq, t = lax.axis_index("seq"), lax.axis_index("tp")
    z, x = seq // nx, seq % nx
    y, c = t // CORES, t % CORES
    rows = nz * nx
    width = r["slot_in"].shape[1]
    started = []

    def at_z(p):
        return (p * nx + x, t)

    def at_xt(p, q):
        return (z * nx + p, q)

    sibling = (seq, y * CORES + 1 - c)

    def copy_to(src, dst, sems, k, device):
        return pltpu.make_async_remote_copy(
            src_ref=src,
            dst_ref=dst,
            send_sem=r[sems + "_s"].at[k],
            recv_sem=r[sems + "_r"].at[k],
            device_id=device,
            device_id_type=MESH,
        )

    def start(*args):
        one = copy_to(*args)
        one.start()
        started.append(one)
        return one

    def exchange(src, dst, sems):
        copies = []
        for k, d in enumerate(far_first(nz)):
            peer = lax.rem(z + d, nz)
            copies.append(start(src.at[peer], dst.at[z], sems, k, at_z(peer)))
        dst[pl.ds(z, 1)] = src[pl.ds(z, 1)]
        return copies

    def arrive(copies):
        for one in copies:
            one.wait_recv()

    inner = r["win_hbm"].shape[0]
    own_inner = pl.ds(pl.multiple_of(c * inner, inner), inner)
    loads = {}
    for k, name in enumerate(("tokens", "cot", "win", "wout")):
        place = r[name].at[own_inner] if name in ("win", "wout") else r[name]
        loads[name] = pltpu.make_async_copy(r[name + "_hbm"], place, r["load"].at[k])
        loads[name].start()

    barrier = pltpu.get_barrier_semaphore()
    peers = [at_z(lax.rem(z + d, nz)) for d in far_first(nz)]
    for d in range(nx):
        peers += [at_xt(lax.rem(x + d, nx), lax.rem(t + e, nt)) for e in range(nt) if d or e]
    for peer in peers:
        pl.semaphore_signal(barrier, inc=1, device_id=peer, device_id_type=MESH)

    loads["tokens"].wait()
    logits = dot(r["embed"][...], r["tokens"][...], (1, 1))
    column_exp = jnp.exp(logits - jnp.max(logits, axis=1, keepdims=True))
    dispatch = column_exp / jnp.sum(column_exp, axis=1, keepdims=True)
    r["dispatch"][...] = dispatch
    slot_in = dot(dispatch.astype(BF16), r["tokens"][...])
    r["slot_in"][...] = slot_in
    scale = lax.rsqrt(jnp.mean(slot_in * slot_in, axis=1, keepdims=True) + 1e-06)
    r["z_out_f"][...] = (slot_in * scale).reshape(nz, nx, width).astype(BF16)
    pl.semaphore_wait(barrier, len(peers))
    z_f = exchange(r["z_out_f"], r["z_in_f"], "z_f")
    row_exp = jnp.exp(logits - jnp.max(logits, axis=0, keepdims=True))
    combine = row_exp / jnp.sum(row_exp, axis=0, keepdims=True)
    r["combine"][...] = combine
    loads["cot"].wait()
    slot_grad = dot(combine.astype(BF16), r["cot"][...])
    r["z_out_b"][...] = slot_grad.reshape(nz, nx, width).astype(BF16)

    plane = [(d, e) for d in range(nx) for e in range(ny)]
    plane.sort(key=lambda step: -min(step[0], nx - step[0]) - min(step[1], ny - step[1]))

    def spread(h, copies):
        arrive(copies)
        held = r["z_in_" + h][...].reshape(rows, width)
        r["x_out_" + h][...] = dot(one_hot_swap(nx, nz), held).astype(BF16).reshape(nx, nz, width)
        mine = r["gather_" + h].at[y, x]
        copies = []
        for k, (d, e) in enumerate(plane[:-1]):
            p, q = lax.rem(x + d, nx), lax.rem(y + e, ny)
            copies.append(start(r["x_out_" + h].at[p], mine, "xy_" + h, k, at_xt(p, q * CORES + c)))
        mine[...] = r["x_out_" + h][x]
        return copies

    def expert(h, copies):
        arrive(copies)
        held = r["gather_" + h][...].reshape(ny * rows, width)
        if h == "f":
            hidden, slope = gelu_and_slope(dot(held, r["win"][...], (1, 1)))
            r["slope"][...] = slope
            weight = r["wout"]
        else:
            hidden = dot(held, r["wout"][...], (1, 1)) * r["slope"][...]
            weight = r["win"]
        hidden = hidden.astype(BF16)
        for low in range(0, width, WIDE):
            cols = pl.ds(low, min(WIDE, width - low))
            part = dot(hidden, weight[:, cols])
            r["part_" + h][:, :, :, cols] = part.astype(BF16).reshape(ny, nx, nz, -1)
        mine = r["sum_" + h].at[y, x]
        copies = []
        for k, (d, e) in enumerate(plane[:-1]):
            p, q = lax.rem(x + d, nx), lax.rem(y + e, ny)
            copies.append(start(r["part_" + h].at[q, p], mine, "sum_" + h, k, at_xt(p, q * CORES + c)))
        mine[...] = r["part_" + h][y, x]
        return copies

    def give_back(h, copies):
        arrive(copies)
        total = r["sum_" + h][0].astype(F32)
        for k in range(1, ny):
            total = total + r["sum_" + h][k].astype(F32)
        held = total.astype(BF16).reshape(rows, width)
        r["z_back_" + h][...] = dot(one_hot_swap(nz, nx), held).reshape(nz, nx, width).astype(BF16)
        return exchange(r["z_back_" + h], r["z_home_" + h], "zh_" + h)

    z_b = exchange(r["z_out_b"], r["z_in_b"], "z_b")
    weights = []
    for k, name in enumerate(("win", "wout")):
        weights.append(start(r[name + "_hbm"], r[name].at[own_inner], "weight", k, sibling))
    xy_f = spread("f", z_f)
    xy_b = spread("b", z_b)
    loads["win"].wait()
    loads["wout"].wait()
    arrive(weights)
    sum_f = expert("f", xy_f)
    sum_b = expert("b", xy_b)
    zh_f = give_back("f", sum_f)
    zh_b = give_back("b", sum_b)

    arrive(zh_f)
    combine = r["combine"][...]
    slot_out = r["z_home_f"][...].reshape(rows, width)
    r["out_left"][...] = combine.T.astype(BF16)
    r["out_right"][...] = slot_out
    grad_combine = dot(slot_out, r["cot"][...], (1, 1))
    combine_inner = jnp.sum(combine * grad_combine, axis=0, keepdims=True)
    grad_logits = combine * (grad_combine - combine_inner)
    slot_in = r["slot_in"][...]
    scale = lax.rsqrt(jnp.mean(slot_in * slot_in, axis=1, keepdims=True) + 1e-06)
    arrive(zh_b)
    grad_normed = r["z_home_b"][...].reshape(rows, width).astype(F32)
    along = jnp.mean(grad_normed * slot_in, axis=1, keepdims=True)
    grad_slot_in = (scale * grad_normed - slot_in * (scale * scale * scale * along)).astype(BF16)
    dispatch = r["dispatch"][...]
    grad_dispatch = dot(grad_slot_in, r["tokens"][...], (1, 1))
    dispatch_inner = jnp.sum(dispatch * grad_dispatch, axis=1, keepdims=True)
    grad_logits = (grad_logits + dispatch * (grad_dispatch - dispatch_inner)).astype(BF16)

    by_x = dot(one_hot_swap(nx, nz), grad_logits).astype(BF16)
    embed_part = dot(by_x, r["tokens"][...]).astype(BF16).reshape(nx, nz, width)
    part = width // nt
    for k in range(nt):
        r["ge_out"][:, k] = embed_part[:, :, k * part : (k + 1) * part]
    ge_xt = []
    mine = r["ge_in"].at[x, t]
    steps = [(d, e) for d in range(nx) for e in range(nt) if d or e]
    for k, (d, e) in enumerate(steps):
        p, q = lax.rem(x + d, nx), lax.rem(t + e, nt)
        ge_xt.append(start(r["ge_out"].at[p, q], mine, "ge_xt", k, at_xt(p, q)))
    mine[...] = r["ge_out"][x, t]
    tok_left = jnp.concatenate([dispatch.astype(BF16).astype(F32), grad_logits.astype(F32)], axis=0)
    r["tok_left"][...] = tok_left.T.astype(BF16)
    r["tok_right"][pl.ds(0, rows)] = grad_slot_in
    r["tok_right"][pl.ds(rows, rows)] = r["embed"][...]
    arrive(ge_xt)
    total = jnp.sum(r["ge_in"][...].astype(F32), axis=(0, 1))
    r["ge_z_out"][...] = total.reshape(nz, 1, part)
    ge_z = exchange(r["ge_z_out"], r["ge_z_in"], "ge_z")
    arrive(ge_z)
    r["gemb"][...] = jnp.sum(r["ge_z_in"][...], axis=0)
    for one in started:
        one.wait_send()


def write_kernel(out_left, out_right, tok_left, tok_right, gemb, out, gtok, gemb_out):
    out[...] = dot(out_left[...], out_right[...]).astype(BF16)
    gtok[...] = dot(tok_left[...], tok_right[...]).astype(BF16)
    gemb_out[...] = gemb[...]


def solution(mesh):
    nx = X_CHIPS if mesh.shape["seq"] % X_CHIPS == 0 else 1
    nz = mesh.shape["seq"] // nx
    nt = mesh.shape["tp"]
    ny = nt // CORES
    rows = nz * nx

    def shards(tokens, slot_embed, w_in, w_out, cotangent):
        patches, width = tokens.shape
        inner = w_out.shape[1]
        vmem, dma = pltpu.VMEM, pltpu.SemaphoreType.DMA
        scratch = dict(
            tokens=vmem((patches, width), BF16),
            cot=vmem((patches, width), BF16),
            win=vmem((CORES * inner, width), BF16),
            wout=vmem((CORES * inner, width), BF16),
            dispatch=vmem((rows, patches), F32),
            combine=vmem((rows, patches), F32),
            slot_in=vmem((rows, width), F32),
            slope=vmem((ny * rows, CORES * inner), F32),
            ge_out=vmem((nx, nt, nz, width // nt), BF16),
            ge_in=vmem((nx, nt, nz, width // nt), BF16),
            ge_z_out=vmem((nz, 1, width // nt), F32),
            ge_z_in=vmem((nz, 1, width // nt), F32),
            load=dma((4,)),
            weight_s=dma((2,)),
            weight_r=dma((2,)),
            ge_xt_s=dma((nx * nt - 1,)),
            ge_xt_r=dma((nx * nt - 1,)),
            ge_z_s=dma((nz - 1,)),
            ge_z_r=dma((nz - 1,)),
        )
        for h in "fb":
            for name in ("z_out", "z_in", "z_back", "z_home"):
                scratch[name + "_" + h] = vmem((nz, nx, width), BF16)
            scratch["x_out_" + h] = vmem((nx, nz, width), BF16)
            for name in ("gather", "part", "sum"):
                scratch[name + "_" + h] = vmem((ny, nx, nz, width), BF16)
            counts = dict(z=nz - 1, zh=nz - 1, xy=nx * ny - 1, sum=nx * ny - 1)
            for name, count in counts.items():
                scratch[name + "_" + h + "_s"] = dma((count,))
                scratch[name + "_" + h + "_r"] = dma((count,))
        ins = ["tokens_hbm", "embed", "win_hbm", "wout_hbm", "cot_hbm"]
        outs = ["out_left", "out_right", "tok_left", "tok_right", "gemb"]
        names = ins + outs + list(scratch)
        anywhere = pl.BlockSpec(memory_space=pl.ANY)
        local = pl.BlockSpec(memory_space=pltpu.VMEM)
        made = pl.pallas_call(
            functools.partial(kernel, names, (nz, nx, ny)),
            out_shape=(
                jax.ShapeDtypeStruct((patches, rows), BF16),
                jax.ShapeDtypeStruct((rows, width), BF16),
                jax.ShapeDtypeStruct((patches, 2 * rows), BF16),
                jax.ShapeDtypeStruct((2 * rows, width), BF16),
                jax.ShapeDtypeStruct((1, width // nt), F32),
            ),
            in_specs=[anywhere, local, anywhere, anywhere, anywhere],
            out_specs=(local,) * 5,
            scratch_shapes=list(scratch.values()),
            compiler_params=pltpu.CompilerParams(
                collective_id=0, has_side_effects=True, vmem_limit_bytes=60 * 1024 * 1024
            ),
        )(tokens, slot_embed, jnp.swapaxes(w_in[0], 0, 1), w_out[0], cotangent)
        step = patches // STEPS
        whole = lambda array: pl.BlockSpec(array.shape, lambda i: (0, 0))
        band = lambda columns: pl.BlockSpec((step, columns), lambda i: (i, 0))
        return pl.pallas_call(
            write_kernel,
            grid=(STEPS,),
            in_specs=[band(rows), whole(made[1]), band(2 * rows), whole(made[3]), whole(made[4])],
            out_specs=(band(width), band(width), whole(made[4])),
            out_shape=(
                jax.ShapeDtypeStruct(tokens.shape, BF16),
                jax.ShapeDtypeStruct(tokens.shape, BF16),
                jax.ShapeDtypeStruct((1, width // nt), F32),
            ),
            compiler_params=pltpu.CompilerParams(vmem_limit_bytes=60 * 1024 * 1024),
        )(*made)

    return jax.shard_map(
        shards,
        mesh=mesh,
        in_specs=(
            P(("seq", "tp"), None),
            P(),
            P("seq", None, "tp"),
            P("seq", "tp", None),
            P(("seq", "tp"), None),
        ),
        out_specs=(P(("seq", "tp"), None), P(("seq", "tp"), None), P("seq", "tp")),
        check_vma=False,
    )
```

```python
import functools
import math

import jax
import jax.numpy as jnp
from jax import lax
from jax.experimental import pallas as pl
from jax.experimental.pallas import tpu as pltpu
from jax.sharding import PartitionSpec as P

X_CHIPS = 4
CORES = 2
WIDE = 256
STEPS = 2
MESH = pl.DeviceIdType.MESH
F32 = jnp.float32
BF16 = jnp.bfloat16


def dot(a, b, contract=(1, 0)):
    dims = (((contract[0],), (contract[1],)), ((), ()))
    return lax.dot_general(a, b, dims, preferred_element_type=F32)


def one_hot_swap(outer, inner):
    count = outer * inner
    row = lax.broadcasted_iota(jnp.int32, (count, count), 0)
    column = lax.broadcasted_iota(jnp.int32, (count, count), 1)
    o, i = row // inner, row % inner
    return (column == i * outer + o).astype(F32).astype(BF16)


def gelu_and_slope(u):
    k = math.sqrt(2.0 / math.pi)
    th = jnp.tanh(k * (u + 0.044715 * (u * u * u)))
    half = 0.5 * (1.0 + th)
    slope = half + 0.5 * u * (1.0 - th * th) * (k * (1.0 + 3 * 0.044715 * (u * u)))
    return u * half, slope


def far_first(count):
    return sorted(range(1, count), key=lambda d: -min(d, count - d))


def kernel(names, sizes, *refs):
    nz, nx, ny = sizes
    nt = CORES * ny
    r = dict(zip(names, refs))
    seq, t = lax.axis_index("seq"), lax.axis_index("tp")
    z, x = seq // nx, seq % nx
    y, c = t // CORES, t % CORES
    rows = nz * nx
    width = r["slot_in"].shape[1]
    started = []

    def at_z(p):
        return (p * nx + x, t)

    def at_xt(p, q):
        return (z * nx + p, q)

    sibling = (seq, y * CORES + 1 - c)

    def copy_to(src, dst, sems, k, device):
        return pltpu.make_async_remote_copy(
            src_ref=src,
            dst_ref=dst,
            send_sem=r[sems + "_s"].at[k],
            recv_sem=r[sems + "_r"].at[k],
            device_id=device,
            device_id_type=MESH,
        )

    def start(*args):
        one = copy_to(*args)
        one.start()
        started.append(one)
        return one

    def exchange(src, dst, sems):
        copies = []
        for k, d in enumerate(far_first(nz)):
            peer = lax.rem(z + d, nz)
            copies.append(start(src.at[peer], dst.at[z], sems, k, at_z(peer)))
        dst[pl.ds(z, 1)] = src[pl.ds(z, 1)]
        return copies

    def arrive(copies):
        for one in copies:
            one.wait_recv()

    inner = r["win_hbm"].shape[0]
    own_inner = pl.ds(pl.multiple_of(c * inner, inner), inner)
    loads = {}
    for k, name in enumerate(("tokens", "cot", "win", "wout")):
        place = r[name].at[own_inner] if name in ("win", "wout") else r[name]
        loads[name] = pltpu.make_async_copy(r[name + "_hbm"], place, r["load"].at[k])
        loads[name].start()

    barrier = pltpu.get_barrier_semaphore()
    peers = [at_z(lax.rem(z + d, nz)) for d in far_first(nz)]
    peers += [at_xt(lax.rem(x + d, nx), lax.rem(y + e, ny) * CORES + c) for d in range(nx) for e in range(ny) if d or e]
    peers += [sibling]
    for peer in peers:
        pl.semaphore_signal(barrier, inc=1, device_id=peer, device_id_type=MESH)

    loads["tokens"].wait()
    logits = dot(r["embed"][...], r["tokens"][...], (1, 1))
    column_exp = jnp.exp(logits - jnp.max(logits, axis=1, keepdims=True))
    dispatch = column_exp / jnp.sum(column_exp, axis=1, keepdims=True)
    r["dispatch"][...] = dispatch
    slot_in = dot(dispatch.astype(BF16), r["tokens"][...])
    r["slot_in"][...] = slot_in
    scale = lax.rsqrt(jnp.mean(slot_in * slot_in, axis=1, keepdims=True) + 1e-06)
    r["z_out_f"][...] = (slot_in * scale).reshape(nz, nx, width).astype(BF16)
    pl.semaphore_wait(barrier, len(peers))
    z_f = exchange(r["z_out_f"], r["z_in_f"], "z_f")
    row_exp = jnp.exp(logits - jnp.max(logits, axis=0, keepdims=True))
    combine = row_exp / jnp.sum(row_exp, axis=0, keepdims=True)
    r["combine"][...] = combine
    loads["cot"].wait()
    slot_grad = dot(combine.astype(BF16), r["cot"][...])
    r["z_out_b"][...] = slot_grad.reshape(nz, nx, width).astype(BF16)

    right, left, across = lax.rem(y + 1, ny), lax.rem(y + ny - 1, ny), lax.rem(y + 2, ny)
    sides = ((0, 1, right, left), (1, ny - 1, left, right))
    half = width // 2
    plane = [(d, e) for d in range(nx) for e in range(ny)]
    plane.sort(key=lambda step: -min(step[0], nx - step[0]) - min(step[1], ny - step[1]))

    def row_of_chips(h, src, peer_y, dst, sems, k):
        copies = []
        for d in range(nx):
            p = lax.rem(x + d, nx)
            if d or peer_y is not y:
                copies.append(start(src.at[p], dst.at[x], sems + h, k + d, at_xt(p, peer_y * CORES + c)))
        return copies

    def spread(h, copies):
        arrive(copies)
        held = r["z_in_" + h][...].reshape(rows, width)
        r["x_out_" + h][...] = dot(one_hot_swap(nx, nz), held).astype(BF16).reshape(nx, nz, width)
        mine = r["gather_" + h].at[y]
        near = [row_of_chips(h, r["x_out_" + h], peer, mine, "xy_", nx * k) for k, _, peer, _ in sides]
        same = row_of_chips(h, r["x_out_" + h], y, mine, "xy_", 2 * nx)
        mine[pl.ds(x, 1)] = r["x_out_" + h][pl.ds(x, 1)]
        return near, same

    def spread_on(h, near):
        copies = []
        for k, _, peer, source in sides:
            arrive(near[k])
            block = r["gather_" + h].at[source, :, :, pl.ds(k * half, half)]
            copies.append(start(block, block, "xy_" + h, 3 * nx + k, at_xt(x, peer * CORES + c)))
        return copies

    def expert(h, copies):
        arrive(copies)
        held = r["gather_" + h][...].reshape(ny * rows, width)
        if h == "f":
            hidden, slope = gelu_and_slope(dot(held, r["win"][...], (1, 1)))
            r["slope"][...] = slope
            weight = r["wout"]
        else:
            hidden = dot(held, r["wout"][...], (1, 1)) * r["slope"][...]
            weight = r["win"]
        hidden = hidden.astype(BF16)
        for low in range(0, width, WIDE):
            cols = pl.ds(low, min(WIDE, width - low))
            part = dot(hidden, weight[:, cols])
            r["part_" + h][:, :, :, cols] = part.astype(BF16).reshape(ny, nx, nz, -1)
        copies = []
        for k, _, peer, _ in sides:
            block = r["part_" + h].at[across, :, :, pl.ds(k * half, half)]
            copies.append(start(block, r["via_" + h].at[k], "sum_" + h, 3 * nx + k, at_xt(x, peer * CORES + c)))
        mine = r["sum_" + h].at[0]
        same = row_of_chips(h, r["part_" + h].at[y], y, mine, "sum_", 2 * nx)
        mine[pl.ds(x, 1)] = r["part_" + h][y, pl.ds(x, 1)]
        return copies, same

    def sum_on(h, copies):
        near = []
        for k, _, peer, _ in sides:
            arrive([copies[k]])
            block = r["part_" + h].at[peer, :, :, pl.ds(k * half, half)]
            block[...] = (block[...].astype(F32) + r["via_" + h][k].astype(F32)).astype(BF16)
            near += row_of_chips(h, r["part_" + h].at[peer], peer, r["sum_" + h].at[1 + k], "sum_", nx * k)
        return near

    def give_back(h, copies):
        arrive(copies)
        total = r["sum_" + h][0].astype(F32)
        for k in range(1, 3):
            total = total + r["sum_" + h][k].astype(F32)
        held = total.astype(BF16).reshape(rows, width)
        r["z_back_" + h][...] = dot(one_hot_swap(nz, nx), held).reshape(nz, nx, width).astype(BF16)
        return exchange(r["z_back_" + h], r["z_home_" + h], "zh_" + h)

    weights = []
    for k, name in enumerate(("win", "wout")):
        weights.append(start(r[name + "_hbm"], r[name].at[own_inner], "weight", k, sibling))
    for one in z_f:
        one.wait_send()
        started.remove(one)
    z_b = exchange(r["z_out_b"], r["z_in_b"], "z_b")
    near_f, same_f = spread("f", z_f)
    on_f = spread_on("f", near_f)
    near_b, same_b = spread("b", z_b)
    loads["win"].wait()
    loads["wout"].wait()
    arrive(weights)
    via_f, home_f = expert("f", same_f + on_f)
    on_b = spread_on("b", near_b)
    home_f += sum_on("f", via_f)
    via_b, home_b = expert("b", same_b + on_b)
    zh_f = give_back("f", home_f)
    home_b += sum_on("b", via_b)
    zh_b = give_back("b", home_b)

    arrive(zh_f)
    combine = r["combine"][...]
    slot_out = r["z_home_f"][...].reshape(rows, width)
    r["out_left"][...] = combine.T.astype(BF16)
    r["out_right"][...] = slot_out
    grad_combine = dot(slot_out, r["cot"][...], (1, 1))
    combine_inner = jnp.sum(combine * grad_combine, axis=0, keepdims=True)
    grad_logits = combine * (grad_combine - combine_inner)
    slot_in = r["slot_in"][...]
    scale = lax.rsqrt(jnp.mean(slot_in * slot_in, axis=1, keepdims=True) + 1e-06)
    arrive(zh_b)
    grad_normed = r["z_home_b"][...].reshape(rows, width).astype(F32)
    along = jnp.mean(grad_normed * slot_in, axis=1, keepdims=True)
    grad_slot_in = (scale * grad_normed - slot_in * (scale * scale * scale * along)).astype(BF16)
    dispatch = r["dispatch"][...]
    grad_dispatch = dot(grad_slot_in, r["tokens"][...], (1, 1))
    dispatch_inner = jnp.sum(dispatch * grad_dispatch, axis=1, keepdims=True)
    grad_logits = (grad_logits + dispatch * (grad_dispatch - dispatch_inner)).astype(BF16)

    by_x = dot(one_hot_swap(nx, nz), grad_logits).astype(BF16)
    embed_part = dot(by_x, r["tokens"][...]).astype(BF16)
    part = width // nt
    for k in range(nt):
        r["ge_core"][k % CORES, k // CORES] = embed_part[:, k * part : (k + 1) * part]
    ge_core = start(r["ge_core"].at[1 - c], r["ge_core_in"], "ge_core", 0, sibling)
    tok_left = jnp.concatenate([dispatch.astype(BF16).astype(F32), grad_logits.astype(F32)], axis=0)
    r["tok_left"][...] = tok_left.T.astype(BF16)
    r["tok_right"][pl.ds(0, rows)] = grad_slot_in
    r["tok_right"][pl.ds(rows, rows)] = r["embed"][...]
    arrive([ge_core])
    pair = r["ge_core"][c].astype(F32) + r["ge_core_in"][...].astype(F32)
    r["ge_out"][...] = pair.astype(BF16).reshape(ny, nx, nz, part)
    ge_xy = []
    mine = r["ge_in"].at[y, x]
    for k, (d, e) in enumerate(plane[:-1]):
        p, q = lax.rem(x + d, nx), lax.rem(y + e, ny)
        ge_xy.append(start(r["ge_out"].at[q, p], mine, "ge_xy", k, at_xt(p, q * CORES + c)))
    mine[...] = r["ge_out"][y, x]
    arrive(ge_xy)
    total = jnp.sum(r["ge_in"][...].astype(F32), axis=(0, 1))
    r["ge_z_out"][...] = total.reshape(nz, 1, part)
    ge_z = exchange(r["ge_z_out"], r["ge_z_in"], "ge_z")
    arrive(ge_z)
    r["gemb"][...] = jnp.sum(r["ge_z_in"][...], axis=0)
    for one in started:
        one.wait_send()


def write_kernel(out_left, out_right, tok_left, tok_right, gemb, out, gtok, gemb_out):
    out[...] = dot(out_left[...], out_right[...]).astype(BF16)
    gtok[...] = dot(tok_left[...], tok_right[...]).astype(BF16)
    gemb_out[...] = gemb[...]


def solution(mesh):
    nx = X_CHIPS if mesh.shape["seq"] % X_CHIPS == 0 else 1
    nz = mesh.shape["seq"] // nx
    nt = mesh.shape["tp"]
    ny = nt // CORES
    rows = nz * nx

    def shards(tokens, slot_embed, w_in, w_out, cotangent):
        patches, width = tokens.shape
        inner = w_out.shape[1]
        vmem, dma = pltpu.VMEM, pltpu.SemaphoreType.DMA
        scratch = dict(
            tokens=vmem((patches, width), BF16),
            cot=vmem((patches, width), BF16),
            win=vmem((CORES * inner, width), BF16),
            wout=vmem((CORES * inner, width), BF16),
            dispatch=vmem((rows, patches), F32),
            combine=vmem((rows, patches), F32),
            slot_in=vmem((rows, width), F32),
            slope=vmem((ny * rows, CORES * inner), F32),
            ge_core=vmem((CORES, ny, rows, width // nt), BF16),
            ge_core_in=vmem((ny, rows, width // nt), BF16),
            ge_out=vmem((ny, nx, nz, width // nt), BF16),
            ge_in=vmem((ny, nx, nz, width // nt), BF16),
            ge_z_out=vmem((nz, 1, width // nt), F32),
            ge_z_in=vmem((nz, 1, width // nt), F32),
            load=dma((4,)),
            weight_s=dma((2,)),
            weight_r=dma((2,)),
            ge_core_s=dma((1,)),
            ge_core_r=dma((1,)),
            ge_xy_s=dma((nx * ny - 1,)),
            ge_xy_r=dma((nx * ny - 1,)),
            ge_z_s=dma((nz - 1,)),
            ge_z_r=dma((nz - 1,)),
        )
        for h in "fb":
            for name in ("z_out", "z_in", "z_back", "z_home"):
                scratch[name + "_" + h] = vmem((nz, nx, width), BF16)
            scratch["x_out_" + h] = vmem((nx, nz, width), BF16)
            for name in ("gather", "part"):
                scratch[name + "_" + h] = vmem((ny, nx, nz, width), BF16)
            scratch["sum_" + h] = vmem((3, nx, nz, width), BF16)
            scratch["via_" + h] = vmem((2, nx, nz, width // 2), BF16)
            counts = dict(z=nz - 1, zh=nz - 1, xy=3 * nx + 2, sum=3 * nx + 2)
            for name, count in counts.items():
                scratch[name + "_" + h + "_s"] = dma((count,))
                scratch[name + "_" + h + "_r"] = dma((count,))
        ins = ["tokens_hbm", "embed", "win_hbm", "wout_hbm", "cot_hbm"]
        outs = ["out_left", "out_right", "tok_left", "tok_right", "gemb"]
        names = ins + outs + list(scratch)
        anywhere = pl.BlockSpec(memory_space=pl.ANY)
        local = pl.BlockSpec(memory_space=pltpu.VMEM)
        made = pl.pallas_call(
            functools.partial(kernel, names, (nz, nx, ny)),
            out_shape=(
                jax.ShapeDtypeStruct((patches, rows), BF16),
                jax.ShapeDtypeStruct((rows, width), BF16),
                jax.ShapeDtypeStruct((patches, 2 * rows), BF16),
                jax.ShapeDtypeStruct((2 * rows, width), BF16),
                jax.ShapeDtypeStruct((1, width // nt), F32),
            ),
            in_specs=[anywhere, local, anywhere, anywhere, anywhere],
            out_specs=(local,) * 5,
            scratch_shapes=list(scratch.values()),
            compiler_params=pltpu.CompilerParams(
                collective_id=0, has_side_effects=True, vmem_limit_bytes=60 * 1024 * 1024
            ),
        )(tokens, slot_embed, jnp.swapaxes(w_in[0], 0, 1), w_out[0], cotangent)
        step = patches // STEPS
        whole = lambda array: pl.BlockSpec(array.shape, lambda i: (0, 0))
        band = lambda columns: pl.BlockSpec((step, columns), lambda i: (i, 0))
        return pl.pallas_call(
            write_kernel,
            grid=(STEPS,),
            in_specs=[band(rows), whole(made[1]), band(2 * rows), whole(made[3]), whole(made[4])],
            out_specs=(band(width), band(width), whole(made[4])),
            out_shape=(
                jax.ShapeDtypeStruct(tokens.shape, BF16),
                jax.ShapeDtypeStruct(tokens.shape, BF16),
                jax.ShapeDtypeStruct((1, width // nt), F32),
            ),
            compiler_params=pltpu.CompilerParams(vmem_limit_bytes=60 * 1024 * 1024),
        )(*made)

    return jax.shard_map(
        shards,
        mesh=mesh,
        in_specs=(
            P(("seq", "tp"), None),
            P(),
            P("seq", None, "tp"),
            P("seq", "tp", None),
            P(("seq", "tp"), None),
        ),
        out_specs=(P(("seq", "tp"), None), P(("seq", "tp"), None), P("seq", "tp")),
        check_vma=False,
    )
```

```python
import functools
import math

import jax
import jax.numpy as jnp
from jax import lax
from jax.experimental import pallas as pl
from jax.experimental.pallas import tpu as pltpu
from jax.sharding import PartitionSpec as P

X_CHIPS = 4
CORES = 2
WIDE = 256
STEPS = 2
MESH = pl.DeviceIdType.MESH
F32 = jnp.float32
BF16 = jnp.bfloat16


def dot(a, b, contract=(1, 0)):
    dims = (((contract[0],), (contract[1],)), ((), ()))
    return lax.dot_general(a, b, dims, preferred_element_type=F32)


def one_hot_swap(outer, inner):
    count = outer * inner
    row = lax.broadcasted_iota(jnp.int32, (count, count), 0)
    column = lax.broadcasted_iota(jnp.int32, (count, count), 1)
    o, i = row // inner, row % inner
    return (column == i * outer + o).astype(F32).astype(BF16)


def gelu_and_slope(u):
    k = math.sqrt(2.0 / math.pi)
    th = jnp.tanh(k * (u + 0.044715 * (u * u * u)))
    half = 0.5 * (1.0 + th)
    slope = half + 0.5 * u * (1.0 - th * th) * (k * (1.0 + 3 * 0.044715 * (u * u)))
    return u * half, slope


def far_first(count):
    return sorted(range(1, count), key=lambda d: -min(d, count - d))


def kernel(names, sizes, *refs):
    nz, nx, ny = sizes
    nt = CORES * ny
    r = dict(zip(names, refs))
    seq, t = lax.axis_index("seq"), lax.axis_index("tp")
    z, x = seq // nx, seq % nx
    y, c = t // CORES, t % CORES
    rows = nz * nx
    width = r["slot_in"].shape[1]
    started = []

    def at_z(p):
        return (p * nx + x, t)

    def at_xt(p, q):
        return (z * nx + p, q)

    sibling = (seq, y * CORES + 1 - c)

    def copy_to(src, dst, sems, k, device):
        return pltpu.make_async_remote_copy(
            src_ref=src,
            dst_ref=dst,
            send_sem=r[sems + "_s"].at[k],
            recv_sem=r[sems + "_r"].at[k],
            device_id=device,
            device_id_type=MESH,
        )

    def start(*args):
        one = copy_to(*args)
        one.start()
        started.append(one)
        return one

    def exchange(src, dst, sems):
        copies = []
        for k, d in enumerate(far_first(nz)):
            peer = lax.rem(z + d, nz)
            copies.append(start(src.at[peer], dst.at[z], sems, k, at_z(peer)))
        dst[pl.ds(z, 1)] = src[pl.ds(z, 1)]
        return copies

    def arrive(copies):
        for one in copies:
            one.wait_recv()

    inner = r["win_hbm"].shape[0]
    own_inner = pl.ds(pl.multiple_of(c * inner, inner), inner)
    loads = {}
    for k, name in enumerate(("tokens", "cot", "win", "wout")):
        place = r[name].at[own_inner] if name in ("win", "wout") else r[name]
        loads[name] = pltpu.make_async_copy(r[name + "_hbm"], place, r["load"].at[k])
        loads[name].start()

    barrier = pltpu.get_barrier_semaphore()
    peers = [at_z(lax.rem(z + d, nz)) for d in far_first(nz)]
    peers += [at_xt(lax.rem(x + d, nx), lax.rem(y + e, ny) * CORES + c) for d in range(nx) for e in range(ny) if d or e]
    peers += [sibling]
    for peer in peers:
        pl.semaphore_signal(barrier, inc=1, device_id=peer, device_id_type=MESH)

    loads["tokens"].wait()
    logits = dot(r["embed"][...], r["tokens"][...], (1, 1))
    column_exp = jnp.exp(logits - jnp.max(logits, axis=1, keepdims=True))
    dispatch = column_exp / jnp.sum(column_exp, axis=1, keepdims=True)
    r["dispatch"][...] = dispatch
    slot_in = dot(dispatch.astype(BF16), r["tokens"][...])
    r["slot_in"][...] = slot_in
    scale = lax.rsqrt(jnp.mean(slot_in * slot_in, axis=1, keepdims=True) + 1e-06)
    r["z_out_f"][...] = (slot_in * scale).reshape(nz, nx, width).astype(BF16)
    pl.semaphore_wait(barrier, len(peers))
    z_f = exchange(r["z_out_f"], r["z_in_f"], "z_f")
    row_exp = jnp.exp(logits - jnp.max(logits, axis=0, keepdims=True))
    combine = row_exp / jnp.sum(row_exp, axis=0, keepdims=True)
    r["combine"][...] = combine
    loads["cot"].wait()
    slot_grad = dot(combine.astype(BF16), r["cot"][...])
    r["z_out_b"][...] = slot_grad.reshape(nz, nx, width).astype(BF16)

    right, left, across = lax.rem(y + 1, ny), lax.rem(y + ny - 1, ny), lax.rem(y + 2, ny)
    sides = ((0, 1, right, left), (1, ny - 1, left, right))
    half = width // 2
    plane = [(d, e) for d in range(nx) for e in range(ny)]
    plane.sort(key=lambda step: -min(step[0], nx - step[0]) - min(step[1], ny - step[1]))

    def row_of_chips(h, src, peer_y, dst, sems, k):
        copies = []
        for d in range(nx):
            p = lax.rem(x + d, nx)
            if d or peer_y is not y:
                copies.append(start(src.at[p], dst.at[x], sems + h, k + d, at_xt(p, peer_y * CORES + c)))
        return copies

    def spread(h, copies):
        arrive(copies)
        held = r["z_in_" + h][...].reshape(rows, width)
        r["x_out_" + h][...] = dot(one_hot_swap(nx, nz), held).astype(BF16).reshape(nx, nz, width)
        mine = r["gather_" + h].at[y]
        near = [row_of_chips(h, r["x_out_" + h], peer, mine, "xy_", nx * k) for k, _, peer, _ in sides]
        same = row_of_chips(h, r["x_out_" + h], y, mine, "xy_", 2 * nx)
        mine[pl.ds(x, 1)] = r["x_out_" + h][pl.ds(x, 1)]
        return near, same

    def spread_on(h, near):
        copies = []
        for k, _, peer, source in sides:
            arrive(near[k])
            block = r["gather_" + h].at[source, :, :, pl.ds(k * half, half)]
            copies.append(start(block, block, "xy_" + h, 3 * nx + k, at_xt(x, peer * CORES + c)))
        return copies

    def expert(h, copies):
        arrive(copies)
        held = r["gather_" + h][...].reshape(ny * rows, width)
        if h == "f":
            hidden, slope = gelu_and_slope(dot(held, r["win"][...], (1, 1)))
            r["slope"][...] = slope
            weight = r["wout"]
        else:
            hidden = dot(held, r["wout"][...], (1, 1)) * r["slope"][...]
            weight = r["win"]
        hidden = hidden.astype(BF16)
        for low in range(0, width, WIDE):
            cols = pl.ds(low, min(WIDE, width - low))
            part = dot(hidden, weight[:, cols])
            r["part_" + h][:, :, :, cols] = part.astype(BF16).reshape(ny, nx, nz, -1)
        copies = []
        for k, _, peer, _ in sides:
            block = r["part_" + h].at[across, :, :, pl.ds(k * half, half)]
            copies.append(start(block, r["via_" + h].at[k], "sum_" + h, 3 * nx + k, at_xt(x, peer * CORES + c)))
        mine = r["sum_" + h].at[0]
        same = row_of_chips(h, r["part_" + h].at[y], y, mine, "sum_", 2 * nx)
        mine[pl.ds(x, 1)] = r["part_" + h][y, pl.ds(x, 1)]
        return copies, same

    def sum_on(h, copies):
        near = []
        for k, _, peer, _ in sides:
            arrive([copies[k]])
            block = r["part_" + h].at[peer, :, :, pl.ds(k * half, half)]
            block[...] = (block[...].astype(F32) + r["via_" + h][k].astype(F32)).astype(BF16)
            near += row_of_chips(h, r["part_" + h].at[peer], peer, r["sum_" + h].at[1 + k], "sum_", nx * k)
        return near

    def give_back(h, copies):
        arrive(copies)
        total = r["sum_" + h][0].astype(F32)
        for k in range(1, 3):
            total = total + r["sum_" + h][k].astype(F32)
        held = total.astype(BF16).reshape(rows, width)
        r["z_back_" + h][...] = dot(one_hot_swap(nz, nx), held).reshape(nz, nx, width).astype(BF16)
        return exchange(r["z_back_" + h], r["z_home_" + h], "zh_" + h)

    weights = []
    for k, name in enumerate(("win", "wout")):
        weights.append(start(r[name + "_hbm"], r[name].at[own_inner], "weight", k, sibling))
    for one in z_f:
        one.wait_send()
        started.remove(one)
    z_b = exchange(r["z_out_b"], r["z_in_b"], "z_b")
    near_f, same_f = spread("f", z_f)
    on_f = spread_on("f", near_f)
    near_b, same_b = spread("b", z_b)
    loads["win"].wait()
    loads["wout"].wait()
    arrive(weights)
    via_f, home_f = expert("f", same_f + on_f)
    on_b = spread_on("b", near_b)
    home_f += sum_on("f", via_f)
    via_b, home_b = expert("b", same_b + on_b)
    zh_f = give_back("f", home_f)
    home_b += sum_on("b", via_b)
    zh_b = give_back("b", home_b)

    arrive(zh_f)
    combine = r["combine"][...]
    slot_out = r["z_home_f"][...].reshape(rows, width)
    r["out_left"][...] = combine.T.astype(BF16)
    r["out_right"][...] = slot_out
    grad_combine = dot(slot_out, r["cot"][...], (1, 1))
    combine_inner = jnp.sum(combine * grad_combine, axis=0, keepdims=True)
    grad_logits = combine * (grad_combine - combine_inner)
    slot_in = r["slot_in"][...]
    scale = lax.rsqrt(jnp.mean(slot_in * slot_in, axis=1, keepdims=True) + 1e-06)
    arrive(zh_b)
    grad_normed = r["z_home_b"][...].reshape(rows, width).astype(F32)
    along = jnp.mean(grad_normed * slot_in, axis=1, keepdims=True)
    grad_slot_in = (scale * grad_normed - slot_in * (scale * scale * scale * along)).astype(BF16)
    dispatch = r["dispatch"][...]
    grad_dispatch = dot(grad_slot_in, r["tokens"][...], (1, 1))
    dispatch_inner = jnp.sum(dispatch * grad_dispatch, axis=1, keepdims=True)
    grad_logits = (grad_logits + dispatch * (grad_dispatch - dispatch_inner)).astype(BF16)

    by_x = dot(one_hot_swap(nx, nz), grad_logits).astype(BF16)
    embed_part = dot(by_x, r["tokens"][...]).astype(BF16)
    part = width // nt
    for k in range(nt):
        r["ge_core"][k % CORES, k // CORES] = embed_part[:, k * part : (k + 1) * part]
    ge_core = start(r["ge_core"].at[1 - c], r["ge_core_in"], "ge_core", 0, sibling)
    tok_left = jnp.concatenate([dispatch.astype(BF16).astype(F32), grad_logits.astype(F32)], axis=0)
    r["tok_left"][...] = tok_left.T.astype(BF16)
    r["tok_right"][pl.ds(0, rows)] = grad_slot_in
    r["tok_right"][pl.ds(rows, rows)] = r["embed"][...]
    arrive([ge_core])
    pair = r["ge_core"][c].astype(F32) + r["ge_core_in"][...].astype(F32)
    r["ge_out"][...] = pair.astype(BF16).reshape(ny, nx, nz, part)
    ge_xy = []
    mine = r["ge_in"].at[y, x]
    for k, (d, e) in enumerate(plane[:-1]):
        p, q = lax.rem(x + d, nx), lax.rem(y + e, ny)
        ge_xy.append(start(r["ge_out"].at[q, p], mine, "ge_xy", k, at_xt(p, q * CORES + c)))
    mine[...] = r["ge_out"][y, x]
    arrive(ge_xy)
    total = jnp.sum(r["ge_in"][...].astype(F32), axis=(0, 1))
    r["ge_z_out"][...] = total.reshape(nz, 1, part)
    ge_z = exchange(r["ge_z_out"], r["ge_z_in"], "ge_z")
    arrive(ge_z)
    r["gemb"][...] = jnp.sum(r["ge_z_in"][...], axis=0)
    for one in started:
        one.wait_send()


def write_kernel(*refs):
    ins, gemb, outs, gemb_out = refs[:4], refs[4], refs[5:7], refs[7]
    held, made, sems = refs[8:12], refs[12:14], refs[14]
    loads = [pltpu.make_async_copy(a, b, sems.at[k]) for k, (a, b) in enumerate(zip(ins, held))]
    for one in loads:
        one.start()
    stores = [pltpu.make_async_copy(gemb, gemb_out, sems.at[4])]
    stores[0].start()
    step = made[0].shape[0] // STEPS
    for k in range(2):
        loads[2 * k].wait()
        loads[2 * k + 1].wait()
        for i in range(STEPS):
            band = pl.ds(i * step, step)
            made[k][band] = dot(held[2 * k][band], held[2 * k + 1][...]).astype(BF16)
            one = pltpu.make_async_copy(made[k].at[band], outs[k].at[band], sems.at[5 + k * STEPS + i])
            one.start()
            stores.append(one)
    for one in stores:
        one.wait()


def solution(mesh):
    nx = X_CHIPS if mesh.shape["seq"] % X_CHIPS == 0 else 1
    nz = mesh.shape["seq"] // nx
    nt = mesh.shape["tp"]
    ny = nt // CORES
    rows = nz * nx

    def shards(tokens, slot_embed, w_in, w_out, cotangent):
        patches, width = tokens.shape
        inner = w_out.shape[1]
        vmem, dma = pltpu.VMEM, pltpu.SemaphoreType.DMA
        scratch = dict(
            tokens=vmem((patches, width), BF16),
            cot=vmem((patches, width), BF16),
            win=vmem((CORES * inner, width), BF16),
            wout=vmem((CORES * inner, width), BF16),
            dispatch=vmem((rows, patches), F32),
            combine=vmem((rows, patches), F32),
            slot_in=vmem((rows, width), F32),
            slope=vmem((ny * rows, CORES * inner), F32),
            ge_core=vmem((CORES, ny, rows, width // nt), BF16),
            ge_core_in=vmem((ny, rows, width // nt), BF16),
            ge_out=vmem((ny, nx, nz, width // nt), BF16),
            ge_in=vmem((ny, nx, nz, width // nt), BF16),
            ge_z_out=vmem((nz, 1, width // nt), F32),
            ge_z_in=vmem((nz, 1, width // nt), F32),
            load=dma((4,)),
            weight_s=dma((2,)),
            weight_r=dma((2,)),
            ge_core_s=dma((1,)),
            ge_core_r=dma((1,)),
            ge_xy_s=dma((nx * ny - 1,)),
            ge_xy_r=dma((nx * ny - 1,)),
            ge_z_s=dma((nz - 1,)),
            ge_z_r=dma((nz - 1,)),
        )
        for h in "fb":
            for name in ("z_out", "z_in", "z_back", "z_home"):
                scratch[name + "_" + h] = vmem((nz, nx, width), BF16)
            scratch["x_out_" + h] = vmem((nx, nz, width), BF16)
            for name in ("gather", "part"):
                scratch[name + "_" + h] = vmem((ny, nx, nz, width), BF16)
            scratch["sum_" + h] = vmem((3, nx, nz, width), BF16)
            scratch["via_" + h] = vmem((2, nx, nz, width // 2), BF16)
            counts = dict(z=nz - 1, zh=nz - 1, xy=3 * nx + 2, sum=3 * nx + 2)
            for name, count in counts.items():
                scratch[name + "_" + h + "_s"] = dma((count,))
                scratch[name + "_" + h + "_r"] = dma((count,))
        ins = ["tokens_hbm", "embed", "win_hbm", "wout_hbm", "cot_hbm"]
        outs = ["out_left", "out_right", "tok_left", "tok_right", "gemb"]
        names = ins + outs + list(scratch)
        anywhere = pl.BlockSpec(memory_space=pl.ANY)
        local = pl.BlockSpec(memory_space=pltpu.VMEM)
        made = pl.pallas_call(
            functools.partial(kernel, names, (nz, nx, ny)),
            out_shape=(
                jax.ShapeDtypeStruct((patches, rows), BF16),
                jax.ShapeDtypeStruct((rows, width), BF16),
                jax.ShapeDtypeStruct((patches, 2 * rows), BF16),
                jax.ShapeDtypeStruct((2 * rows, width), BF16),
                jax.ShapeDtypeStruct((1, width // nt), F32),
            ),
            in_specs=[anywhere, local, anywhere, anywhere, anywhere],
            out_specs=(local,) * 5,
            scratch_shapes=list(scratch.values()),
            compiler_params=pltpu.CompilerParams(
                collective_id=0, has_side_effects=True, vmem_limit_bytes=60 * 1024 * 1024
            ),
        )(tokens, slot_embed, jnp.swapaxes(w_in[0], 0, 1), w_out[0], cotangent)
        return pl.pallas_call(
            write_kernel,
            in_specs=[anywhere] * 5,
            out_specs=(anywhere,) * 3,
            scratch_shapes=[vmem(array.shape, BF16) for array in made[:4]]
            + [vmem(tokens.shape, BF16)] * 2
            + [dma((5 + 2 * STEPS,))],
            out_shape=(
                jax.ShapeDtypeStruct(tokens.shape, BF16),
                jax.ShapeDtypeStruct(tokens.shape, BF16),
                jax.ShapeDtypeStruct((1, width // nt), F32),
            ),
            compiler_params=pltpu.CompilerParams(vmem_limit_bytes=60 * 1024 * 1024),
        )(*made)

    return jax.shard_map(
        shards,
        mesh=mesh,
        in_specs=(
            P(("seq", "tp"), None),
            P(),
            P("seq", None, "tp"),
            P("seq", "tp", None),
            P(("seq", "tp"), None),
        ),
        out_specs=(P(("seq", "tp"), None), P(("seq", "tp"), None), P("seq", "tp")),
        check_vma=False,
    )
```

```python
import functools
import math

import jax
import jax.numpy as jnp
from jax import lax
from jax.experimental import pallas as pl
from jax.experimental.pallas import tpu as pltpu
from jax.sharding import PartitionSpec as P

X_CHIPS = 4
CORES = 2
WIDE = 256
STEPS = 2
MESH = pl.DeviceIdType.MESH
F32 = jnp.float32
BF16 = jnp.bfloat16


def dot(a, b, contract=(1, 0)):
    dims = (((contract[0],), (contract[1],)), ((), ()))
    return lax.dot_general(a, b, dims, preferred_element_type=F32)


def one_hot_swap(outer, inner):
    count = outer * inner
    row = lax.broadcasted_iota(jnp.int32, (count, count), 0)
    column = lax.broadcasted_iota(jnp.int32, (count, count), 1)
    o, i = row // inner, row % inner
    return (column == i * outer + o).astype(F32).astype(BF16)


def gelu_and_slope(u):
    k = math.sqrt(2.0 / math.pi)
    th = jnp.tanh(k * (u + 0.044715 * (u * u * u)))
    half = 0.5 * (1.0 + th)
    slope = half + 0.5 * u * (1.0 - th * th) * (k * (1.0 + 3 * 0.044715 * (u * u)))
    return u * half, slope


def far_first(count):
    return sorted(range(1, count), key=lambda d: -min(d, count - d))


def kernel(names, sizes, *refs):
    nz, nx, ny = sizes
    nt = CORES * ny
    r = dict(zip(names, refs))
    seq, t = lax.axis_index("seq"), lax.axis_index("tp")
    z, x = seq // nx, seq % nx
    y, c = t // CORES, t % CORES
    rows = nz * nx
    width = r["slot_in"].shape[1]
    started = []

    def at_z(p):
        return (p * nx + x, t)

    def at_xt(p, q):
        return (z * nx + p, q)

    sibling = (seq, y * CORES + 1 - c)

    def copy_to(src, dst, sems, k, device):
        return pltpu.make_async_remote_copy(
            src_ref=src,
            dst_ref=dst,
            send_sem=r[sems + "_s"].at[k],
            recv_sem=r[sems + "_r"].at[k],
            device_id=device,
            device_id_type=MESH,
        )

    def start(*args):
        one = copy_to(*args)
        one.start()
        started.append(one)
        return one

    def exchange(src, dst, sems):
        copies = []
        for k, d in enumerate(far_first(nz)):
            peer = lax.rem(z + d, nz)
            copies.append(start(src.at[peer], dst.at[z], sems, k, at_z(peer)))
        dst[pl.ds(z, 1)] = src[pl.ds(z, 1)]
        return copies

    def arrive(copies):
        for one in copies:
            one.wait_recv()

    inner = r["win_hbm"].shape[0]
    own_inner = pl.ds(pl.multiple_of(c * inner, inner), inner)
    barrier = pltpu.get_barrier_semaphore()
    peers = [at_z(lax.rem(z + d, nz)) for d in far_first(nz)]
    peers += [at_xt(lax.rem(x + d, nx), lax.rem(y + e, ny) * CORES + c) for d in range(nx) for e in range(ny) if d or e]
    peers += [sibling]
    for peer in peers:
        pl.semaphore_signal(barrier, inc=1, device_id=peer, device_id_type=MESH)

    loads = {}
    for k, name in enumerate(("tokens", "cot", "win", "wout")):
        place = r[name].at[own_inner] if name in ("win", "wout") else r[name]
        loads[name] = pltpu.make_async_copy(r[name + "_hbm"], place, r["load"].at[k])
        loads[name].start()

    loads["tokens"].wait()
    logits = dot(r["embed"][...], r["tokens"][...], (1, 1))
    column_exp = jnp.exp(logits - jnp.max(logits, axis=1, keepdims=True))
    dispatch = column_exp / jnp.sum(column_exp, axis=1, keepdims=True)
    r["dispatch"][...] = dispatch
    slot_in = dot(dispatch.astype(BF16), r["tokens"][...])
    r["slot_in"][...] = slot_in
    scale = lax.rsqrt(jnp.mean(slot_in * slot_in, axis=1, keepdims=True) + 1e-06)
    r["z_out_f"][...] = (slot_in * scale).reshape(nz, nx, width).astype(BF16)
    pl.semaphore_wait(barrier, len(peers))
    z_f = exchange(r["z_out_f"], r["z_in_f"], "z_f")
    row_exp = jnp.exp(logits - jnp.max(logits, axis=0, keepdims=True))
    combine = row_exp / jnp.sum(row_exp, axis=0, keepdims=True)
    r["combine"][...] = combine
    loads["cot"].wait()
    slot_grad = dot(combine.astype(BF16), r["cot"][...])
    r["z_out_b"][...] = slot_grad.reshape(nz, nx, width).astype(BF16)

    right, left, across = lax.rem(y + 1, ny), lax.rem(y + ny - 1, ny), lax.rem(y + 2, ny)
    sides = ((0, 1, right, left), (1, ny - 1, left, right))
    half = width // 2
    plane = [(d, e) for d in range(nx) for e in range(ny)]
    plane.sort(key=lambda step: -min(step[0], nx - step[0]) - min(step[1], ny - step[1]))

    def row_of_chips(h, src, peer_y, dst, sems, k):
        copies = []
        for d in range(nx):
            p = lax.rem(x + d, nx)
            if d or peer_y is not y:
                copies.append(start(src.at[p], dst.at[x], sems + h, k + d, at_xt(p, peer_y * CORES + c)))
        return copies

    def spread(h, copies):
        arrive(copies)
        held = r["z_in_" + h][...].reshape(rows, width)
        r["x_out_" + h][...] = dot(one_hot_swap(nx, nz), held).astype(BF16).reshape(nx, nz, width)
        mine = r["gather_" + h].at[y]
        near = [row_of_chips(h, r["x_out_" + h], peer, mine, "xy_", nx * k) for k, _, peer, _ in sides]
        same = row_of_chips(h, r["x_out_" + h], y, mine, "xy_", 2 * nx)
        mine[pl.ds(x, 1)] = r["x_out_" + h][pl.ds(x, 1)]
        return near, same

    def spread_on(h, near):
        copies = []
        for k, _, peer, source in sides:
            arrive(near[k])
            block = r["gather_" + h].at[source, :, :, pl.ds(k * half, half)]
            copies.append(start(block, block, "xy_" + h, 3 * nx + k, at_xt(x, peer * CORES + c)))
        return copies

    def expert(h, copies):
        arrive(copies)
        held = r["gather_" + h][...].reshape(ny * rows, width)
        if h == "f":
            hidden, slope = gelu_and_slope(dot(held, r["win"][...], (1, 1)))
            r["slope"][...] = slope
            weight = r["wout"]
        else:
            hidden = dot(held, r["wout"][...], (1, 1)) * r["slope"][...]
            weight = r["win"]
        hidden = hidden.astype(BF16)
        for low in range(0, width, WIDE):
            cols = pl.ds(low, min(WIDE, width - low))
            part = dot(hidden, weight[:, cols])
            r["part_" + h][:, :, :, cols] = part.astype(BF16).reshape(ny, nx, nz, -1)
        copies = []
        for k, _, peer, _ in sides:
            block = r["part_" + h].at[across, :, :, pl.ds(k * half, half)]
            copies.append(start(block, r["via_" + h].at[k], "sum_" + h, 3 * nx + k, at_xt(x, peer * CORES + c)))
        mine = r["sum_" + h].at[0]
        same = row_of_chips(h, r["part_" + h].at[y], y, mine, "sum_", 2 * nx)
        mine[pl.ds(x, 1)] = r["part_" + h][y, pl.ds(x, 1)]
        return copies, same

    def sum_on(h, copies):
        near = []
        for k, _, peer, _ in sides:
            arrive([copies[k]])
            block = r["part_" + h].at[peer, :, :, pl.ds(k * half, half)]
            block[...] = (block[...].astype(F32) + r["via_" + h][k].astype(F32)).astype(BF16)
            near += row_of_chips(h, r["part_" + h].at[peer], peer, r["sum_" + h].at[1 + k], "sum_", nx * k)
        return near

    def give_back(h, copies):
        arrive(copies)
        total = r["sum_" + h][0].astype(F32)
        for k in range(1, 3):
            total = total + r["sum_" + h][k].astype(F32)
        held = total.astype(BF16).reshape(rows, width)
        r["z_back_" + h][...] = dot(one_hot_swap(nz, nx), held).reshape(nz, nx, width).astype(BF16)
        return exchange(r["z_back_" + h], r["z_home_" + h], "zh_" + h)

    for one in z_f:
        one.wait_send()
        started.remove(one)
    z_b = exchange(r["z_out_b"], r["z_in_b"], "z_b")
    weights = []
    for k, name in enumerate(("win", "wout")):
        weights.append(start(r[name + "_hbm"], r[name].at[own_inner], "weight", k, sibling))
    near_f, same_f = spread("f", z_f)
    on_f = spread_on("f", near_f)
    near_b, same_b = spread("b", z_b)
    loads["win"].wait()
    loads["wout"].wait()
    arrive(weights)
    via_f, home_f = expert("f", same_f + on_f)
    on_b = spread_on("b", near_b)
    home_f += sum_on("f", via_f)
    via_b, home_b = expert("b", same_b + on_b)
    zh_f = give_back("f", home_f)
    home_b += sum_on("b", via_b)
    zh_b = give_back("b", home_b)

    arrive(zh_f)
    combine = r["combine"][...]
    slot_out = r["z_home_f"][...].reshape(rows, width)
    r["out_left"][...] = combine.T.astype(BF16)
    r["out_right"][...] = slot_out
    grad_combine = dot(slot_out, r["cot"][...], (1, 1))
    combine_inner = jnp.sum(combine * grad_combine, axis=0, keepdims=True)
    grad_logits = combine * (grad_combine - combine_inner)
    slot_in = r["slot_in"][...]
    scale = lax.rsqrt(jnp.mean(slot_in * slot_in, axis=1, keepdims=True) + 1e-06)
    arrive(zh_b)
    grad_normed = r["z_home_b"][...].reshape(rows, width).astype(F32)
    along = jnp.mean(grad_normed * slot_in, axis=1, keepdims=True)
    grad_slot_in = (scale * grad_normed - slot_in * (scale * scale * scale * along)).astype(BF16)
    dispatch = r["dispatch"][...]
    grad_dispatch = dot(grad_slot_in, r["tokens"][...], (1, 1))
    dispatch_inner = jnp.sum(dispatch * grad_dispatch, axis=1, keepdims=True)
    grad_logits = (grad_logits + dispatch * (grad_dispatch - dispatch_inner)).astype(BF16)

    by_x = dot(one_hot_swap(nx, nz), grad_logits).astype(BF16)
    embed_part = dot(by_x, r["tokens"][...]).astype(BF16)
    part = width // nt
    for k in range(nt):
        r["ge_core"][k % CORES, k // CORES] = embed_part[:, k * part : (k + 1) * part]
    ge_core = start(r["ge_core"].at[1 - c], r["ge_core_in"], "ge_core", 0, sibling)
    tok_left = jnp.concatenate([dispatch.astype(BF16).astype(F32), grad_logits.astype(F32)], axis=0)
    r["tok_left"][...] = tok_left.T.astype(BF16)
    r["tok_right"][pl.ds(0, rows)] = grad_slot_in
    r["tok_right"][pl.ds(rows, rows)] = r["embed"][...]
    arrive([ge_core])
    pair = r["ge_core"][c].astype(F32) + r["ge_core_in"][...].astype(F32)
    r["ge_out"][...] = pair.astype(BF16).reshape(ny, nx, nz, part)
    ge_xy = []
    mine = r["ge_in"].at[y, x]
    for k, (d, e) in enumerate(plane[:-1]):
        p, q = lax.rem(x + d, nx), lax.rem(y + e, ny)
        ge_xy.append(start(r["ge_out"].at[q, p], mine, "ge_xy", k, at_xt(p, q * CORES + c)))
    mine[...] = r["ge_out"][y, x]
    arrive(ge_xy)
    total = jnp.sum(r["ge_in"][...].astype(F32), axis=(0, 1))
    r["ge_z_out"][...] = total.reshape(nz, 1, part)
    ge_z = exchange(r["ge_z_out"], r["ge_z_in"], "ge_z")
    arrive(ge_z)
    r["gemb"][...] = jnp.sum(r["ge_z_in"][...], axis=0)
    for one in started:
        one.wait_send()


def write_kernel(*refs):
    ins, gemb, outs, gemb_out = refs[:4], refs[4], refs[5:7], refs[7]
    held, made, sems = refs[8:12], refs[12:14], refs[14]
    loads = [pltpu.make_async_copy(a, b, sems.at[k]) for k, (a, b) in enumerate(zip(ins, held))]
    for one in loads:
        one.start()
    stores = [pltpu.make_async_copy(gemb, gemb_out, sems.at[4])]
    stores[0].start()
    step = made[0].shape[0] // STEPS
    for k in range(2):
        loads[2 * k].wait()
        loads[2 * k + 1].wait()
        for i in range(STEPS):
            band = pl.ds(i * step, step)
            made[k][band] = dot(held[2 * k][band], held[2 * k + 1][...]).astype(BF16)
            one = pltpu.make_async_copy(made[k].at[band], outs[k].at[band], sems.at[5 + k * STEPS + i])
            one.start()
            stores.append(one)
    for one in stores:
        one.wait()


def solution(mesh):
    nx = X_CHIPS if mesh.shape["seq"] % X_CHIPS == 0 else 1
    nz = mesh.shape["seq"] // nx
    nt = mesh.shape["tp"]
    ny = nt // CORES
    rows = nz * nx

    def shards(tokens, slot_embed, w_in, w_out, cotangent):
        patches, width = tokens.shape
        inner = w_out.shape[1]
        vmem, dma = pltpu.VMEM, pltpu.SemaphoreType.DMA
        scratch = dict(
            tokens=vmem((patches, width), BF16),
            cot=vmem((patches, width), BF16),
            win=vmem((CORES * inner, width), BF16),
            wout=vmem((CORES * inner, width), BF16),
            dispatch=vmem((rows, patches), F32),
            combine=vmem((rows, patches), F32),
            slot_in=vmem((rows, width), F32),
            slope=vmem((ny * rows, CORES * inner), F32),
            ge_core=vmem((CORES, ny, rows, width // nt), BF16),
            ge_core_in=vmem((ny, rows, width // nt), BF16),
            ge_out=vmem((ny, nx, nz, width // nt), BF16),
            ge_in=vmem((ny, nx, nz, width // nt), BF16),
            ge_z_out=vmem((nz, 1, width // nt), F32),
            ge_z_in=vmem((nz, 1, width // nt), F32),
            load=dma((4,)),
            weight_s=dma((2,)),
            weight_r=dma((2,)),
            ge_core_s=dma((1,)),
            ge_core_r=dma((1,)),
            ge_xy_s=dma((nx * ny - 1,)),
            ge_xy_r=dma((nx * ny - 1,)),
            ge_z_s=dma((nz - 1,)),
            ge_z_r=dma((nz - 1,)),
        )
        for h in "fb":
            for name in ("z_out", "z_in", "z_back", "z_home"):
                scratch[name + "_" + h] = vmem((nz, nx, width), BF16)
            scratch["x_out_" + h] = vmem((nx, nz, width), BF16)
            for name in ("gather", "part"):
                scratch[name + "_" + h] = vmem((ny, nx, nz, width), BF16)
            scratch["sum_" + h] = vmem((3, nx, nz, width), BF16)
            scratch["via_" + h] = vmem((2, nx, nz, width // 2), BF16)
            counts = dict(z=nz - 1, zh=nz - 1, xy=3 * nx + 2, sum=3 * nx + 2)
            for name, count in counts.items():
                scratch[name + "_" + h + "_s"] = dma((count,))
                scratch[name + "_" + h + "_r"] = dma((count,))
        ins = ["tokens_hbm", "embed", "win_hbm", "wout_hbm", "cot_hbm"]
        outs = ["out_left", "out_right", "tok_left", "tok_right", "gemb"]
        names = ins + outs + list(scratch)
        anywhere = pl.BlockSpec(memory_space=pl.ANY)
        local = pl.BlockSpec(memory_space=pltpu.VMEM)
        made = pl.pallas_call(
            functools.partial(kernel, names, (nz, nx, ny)),
            out_shape=(
                jax.ShapeDtypeStruct((patches, rows), BF16),
                jax.ShapeDtypeStruct((rows, width), BF16),
                jax.ShapeDtypeStruct((patches, 2 * rows), BF16),
                jax.ShapeDtypeStruct((2 * rows, width), BF16),
                jax.ShapeDtypeStruct((1, width // nt), F32),
            ),
            in_specs=[anywhere, local, anywhere, anywhere, anywhere],
            out_specs=(local,) * 5,
            scratch_shapes=list(scratch.values()),
            compiler_params=pltpu.CompilerParams(
                collective_id=0, has_side_effects=True, vmem_limit_bytes=60 * 1024 * 1024
            ),
        )(tokens, slot_embed, jnp.swapaxes(w_in[0], 0, 1), w_out[0], cotangent)
        return pl.pallas_call(
            write_kernel,
            in_specs=[anywhere] * 5,
            out_specs=(anywhere,) * 3,
            scratch_shapes=[vmem(array.shape, BF16) for array in made[:4]]
            + [vmem(tokens.shape, BF16)] * 2
            + [dma((5 + 2 * STEPS,))],
            out_shape=(
                jax.ShapeDtypeStruct(tokens.shape, BF16),
                jax.ShapeDtypeStruct(tokens.shape, BF16),
                jax.ShapeDtypeStruct((1, width // nt), F32),
            ),
            compiler_params=pltpu.CompilerParams(vmem_limit_bytes=60 * 1024 * 1024),
        )(*made)

    return jax.shard_map(
        shards,
        mesh=mesh,
        in_specs=(
            P(("seq", "tp"), None),
            P(),
            P("seq", None, "tp"),
            P("seq", "tp", None),
            P(("seq", "tp"), None),
        ),
        out_specs=(P(("seq", "tp"), None), P(("seq", "tp"), None), P("seq", "tp")),
        check_vma=False,
    )
```
